32 devices in a mesh: mp: 4 (over y, x), hidden: 8 (over z, core).
Axes of the slice: x: 2, y: 2, z: 4, core: 2. Of those that a mesh axis runs over, the one named last changes fastest.
Arguments:
- inputs: float32 [64, 8192], P('hidden', 'mp'), may hold values from -6 to 6
- weight: float32 [8192, 32768], P('mp', 'hidden'), may hold values from -0.0625 to 0.0625
- upstream: float32 [64, 32768], P('mp', 'hidden'), may hold values from -6 to 6
Outputs:
- input_grad: float32 [64, 8192], P('hidden', 'mp')
- weight_grad: float32 [8192, 32768], P('mp', 'hidden')
The draws below stay inside these ranges and needn't reach their ends.
All inputs are finite; a program needn't handle non-finite values.
Results may differ from the reference program's by a relative error of at most 0.000092.
Values sent between devices are 32-bit elements; how exact they have to be, the bound alone decides.
No kernel may reach another device: no remote copies, remote signals or barrier semaphores. Data moves between devices by JAX's collectives and lax.ppermute only.
A program may use at most 192 MiB of HBM per device.

```python
import jax
import jax.numpy as jnp
from jax import lax

D = 8192
FF = 32768
ROWS = 64


def block_levels(key, shape, pieces, least, largest):
    level, own = 1.0, jax.random.fold_in(key, 6)
    for dim, shards_of in pieces:
        heights = jnp.exp(jax.random.uniform(jax.random.fold_in(own, dim), (shards_of,), jnp.float32, least / len(pieces), largest / len(pieces)))
        level = level * jnp.repeat(heights, shape[dim] // shards_of).reshape([-1 if axis == dim else 1 for axis in range(len(shape))])
    return level


def normal_values(own_key, shape, scale, reach, pieces=(), kind=jnp.bfloat16):
    array = jax.random.normal(own_key, shape, jnp.float32) * scale
    if len(pieces) > 0:
        array = block_levels(own_key, shape, pieces, -0.22, 0.18) * array
    return jnp.clip(array, min=-reach, max=reach).astype(kind)


def setup_inputs(seed: int = 0) -> dict:
    key_of = jax.random.split(jax.random.key(seed), 4)
    inputs = normal_values(key_of[0], (ROWS, D), 1.0, 6.0, ((0, 8), (1, 4)), jnp.float32)
    weight = normal_values(key_of[1], (D, FF), D ** -0.5, 0.0625, ((0, 4), (1, 8)), jnp.float32)
    upstream = normal_values(key_of[2], (ROWS, FF), 1.0, 6.0, ((0, 4), (1, 8)), jnp.float32)
    return {"inputs": inputs, "weight": weight, "upstream": upstream}


def gelu_slope(pre):
    cdf = 0.5 * (1.0 + jax.scipy.special.erf(pre * 0.7071067811865476))
    return cdf + pre * jnp.exp(-0.5 * pre * pre) * 0.3989422804014327


def reference(inputs, weight, upstream):
    pre = jnp.dot(inputs, weight, preferred_element_type=jnp.float32, precision=lax.Precision.HIGHEST)
    grad_pre = upstream * gelu_slope(pre)
    input_grad = lax.dot_general(grad_pre, weight, (((1,), (1,)), ((), ())), precision=lax.Precision.HIGHEST, preferred_element_type=jnp.float32)
    weight_grad = lax.dot_general(inputs, grad_pre, (((0,), (0,)), ((), ())), precision=lax.Precision.HIGHEST, preferred_element_type=jnp.float32)
    return input_grad, weight_grad
```

```python
import functools

import jax
import jax.numpy as jnp
from jax import lax
from jax.experimental import pallas as pl
from jax.experimental.pallas import tpu as pltpu
from jax.sharding import PartitionSpec as P

F32, BF16 = jnp.float32, jnp.bfloat16
MIB = 1 << 20
VMEM = pl.BlockSpec(memory_space=pltpu.VMEM)
CHUNKS = 2


def params(mib=12):
    return pltpu.CompilerParams(vmem_limit_bytes=mib * MIB)


def cost(flops, moved):
    return pl.CostEstimate(flops=int(flops), bytes_accessed=int(moved), transcendentals=0)


def fit(size, block):
    while size % block:
        block //= 2
    return block


def halves(value):
    high = value.astype(BF16)
    return high, (value - high.astype(F32)).astype(BF16)


def swap(value, axis, mask):
    size = lax.axis_size(axis)
    return lax.ppermute(value, axis, [(i, i ^ mask) for i in range(size)])


def split_kernel(rows, w_ref, high_ref, low_ref):
    at = pl.ds(pl.multiple_of(pl.program_id(0) * rows, rows), rows)
    high, low = halves(w_ref[...])
    high_ref[at, :] = high
    low_ref[at, :] = low


def split_weight(weight):
    deep, wide = weight.shape
    rows = fit(deep, 128)
    return pl.pallas_call(
        functools.partial(split_kernel, rows),
        grid=(deep // rows,),
        in_specs=[pl.BlockSpec((rows, wide), lambda i: (i, 0))],
        out_specs=[VMEM, VMEM],
        out_shape=[pltpu.VMEM((deep, wide), BF16)] * 2,
        compiler_params=params(),
        cost_estimate=cost(0, 8 * deep * wide),
        name="split_weight",
    )(weight)


def rows_kernel(n_mp, n_pair, *refs):
    pieces, (x_ref, flat) = refs[:n_pair], refs[n_pair:]
    pair = pieces[0].shape[0]
    z = lax.axis_index("hidden") // 2
    me = lax.axis_index("mp")
    for mask in range(n_pair):
        flat[pl.ds(pl.multiple_of((z ^ mask) * pair, pair), pair), :] = pieces[mask][...]
    rows = flat.shape[0]
    group = rows // n_mp
    for mask in range(n_mp):
        block = flat[pl.ds(pl.multiple_of((me ^ mask) * group, group), group), :]
        high, low = halves(block)
        x_ref[mask * group : (mask + 1) * group, :] = high
        x_ref[rows + mask * group : rows + (mask + 1) * group, :] = low


def order_rows(pieces, n_mp):
    pair, deep = pieces[0].shape
    rows = pair * len(pieces)
    return pl.pallas_call(
        functools.partial(rows_kernel, n_mp, len(pieces)),
        in_specs=[VMEM] * len(pieces),
        out_specs=VMEM,
        out_shape=jax.ShapeDtypeStruct((2 * rows, deep), BF16),
        scratch_shapes=[pltpu.VMEM((rows, deep), F32)],
        compiler_params=params(),
        cost_estimate=cost(0, 8 * rows * deep),
        name="order_rows",
    )(*pieces)


def turn_kernel(x_ref, t_ref):
    rows = x_ref.shape[0] // 2
    high = x_ref[:rows, :].astype(F32)
    low = x_ref[rows:, :].astype(F32)
    t_ref[...] = jnp.concatenate([high, high, low, low], axis=0).T.astype(BF16)


def turn_rows(x):
    two, deep = x.shape
    return pl.pallas_call(
        turn_kernel,
        in_specs=[VMEM],
        out_specs=VMEM,
        out_shape=jax.ShapeDtypeStruct((deep, 2 * two), BF16),
        compiler_params=params(),
        cost_estimate=cost(0, 4 * two * deep),
        name="turn_rows",
    )(x)


def pre_kernel(n_mp, first, block, x_ref, high_ref, low_ref, *outs):
    rows = x_ref.shape[0] // 2
    group = rows // n_mp

    def step(j, _):
        here = pl.ds(pl.multiple_of(j * block, block), block)
        there = pl.ds(pl.multiple_of(first + j * block, block), block)
        both = jnp.dot(x_ref[...], high_ref[:, there], preferred_element_type=F32)
        last = jnp.dot(x_ref[:rows, :], low_ref[:, there], preferred_element_type=F32)
        total = both[:rows] + both[rows:] + last
        for mask in range(n_mp):
            outs[mask][:, here] = total[mask * group : (mask + 1) * group]
        return 0

    lax.fori_loop(0, outs[0].shape[1] // block, step, 0)


def partial_pre(x, high, low, n_mp, first, count):
    rows, deep = x.shape[0] // 2, x.shape[1]
    return pl.pallas_call(
        functools.partial(pre_kernel, n_mp, first, fit(count, 512)),
        in_specs=[VMEM] * 3,
        out_specs=[VMEM] * n_mp,
        out_shape=[jax.ShapeDtypeStruct((rows // n_mp, count), F32)] * n_mp,
        compiler_params=params(),
        cost_estimate=cost(20 * rows * deep * count, 4 * rows * count),
        name="partial_pre",
    )(x, high, low)


def slope_kernel(first, *refs):
    parts, up_ref, out_ref = refs[:-2], refs[-2], refs[-1]
    pre = parts[0][...]
    for part in parts[1:]:
        pre = pre + part[...]
    cdf = 0.5 * (1.0 + lax.erf(pre * 0.7071067811865476))
    slope = cdf + pre * jnp.exp(-0.5 * pre * pre) * 0.3989422804014327
    out_ref[...] = up_ref[:, first : first + pre.shape[1]] * slope


def grad_mine(parts, upstream, first):
    rows, count = parts[0].shape
    return pl.pallas_call(
        functools.partial(slope_kernel, first),
        in_specs=[VMEM] * (len(parts) + 1),
        out_specs=VMEM,
        out_shape=jax.ShapeDtypeStruct((rows, count), F32),
        compiler_params=params(),
        cost_estimate=cost(0, 24 * rows * count),
        name="grad_mine",
    )(*parts, upstream)


def input_kernel(n_mp, first, block, has_total, is_last, high_ref, low_ref, *refs):
    pieces, refs = refs[:n_mp], refs[n_mp:]
    if has_total:
        total_ref, refs = refs[0], refs[1:]
    outs, (stack,) = refs[:-1], refs[-1:]
    group, count = pieces[0].shape
    rows = group * n_mp
    for mask in range(n_mp):
        at = slice(mask * group, (mask + 1) * group)
        high, low = halves(pieces[mask][...])
        stack[:, at] = high.astype(F32).T.astype(BF16)
        stack[:, rows + mask * group : rows + (mask + 1) * group] = low.astype(F32).T.astype(BF16)
    cols = slice(first, first + count)
    me = lax.axis_index("mp")
    hid = lax.axis_index("hidden")
    if is_last:
        keep_ref, send_ref, flat = outs
    else:
        (flat,) = outs

    def step(j, _):
        here = pl.ds(pl.multiple_of(j * block, block), block)
        both = jnp.dot(high_ref[here, cols], stack[...], preferred_element_type=F32)
        last = jnp.dot(low_ref[here, cols], stack[:, :rows], preferred_element_type=F32)
        total = (both[:, :rows] + both[:, rows:] + last).T
        if has_total:
            total = total + total_ref[:, here]
        if not is_last:
            flat[:, here] = total
            return 0
        for mask in range(n_mp):
            place = pl.ds(pl.multiple_of((me ^ mask) * group, group), group)
            flat[place, :] = total[mask * group : (mask + 1) * group]
        n_pair, size = keep_ref.shape[0], keep_ref.shape[1]
        for mask in range(n_pair):
            own = hid ^ (2 * mask)
            keep_ref[mask, :, here] = flat[pl.ds(pl.multiple_of(own * size, size), size), :]
            other = own ^ 1
            send_ref[mask, :, here] = flat[pl.ds(pl.multiple_of(other * size, size), size), :]
        return 0

    lax.fori_loop(0, high_ref.shape[0] // block, step, 0)


def input_share(high, low, pieces, total, first, n_hid, is_last):
    n_mp = len(pieces)
    group, count = pieces[0].shape
    rows, deep = group * n_mp, high.shape[0]
    block = fit(deep, 512)
    has_total = total is not None
    ins = [high, low, *pieces] + ([total] if has_total else [])
    scratch = [pltpu.VMEM((count, 2 * rows), BF16)]
    if is_last:
        one = jax.ShapeDtypeStruct((n_hid // 2, rows // n_hid, deep), F32)
        shapes = [one, one]
        scratch = [pltpu.VMEM((rows, block), F32)] + scratch
    else:
        shapes = [jax.ShapeDtypeStruct((rows, deep), F32)]
    return pl.pallas_call(
        functools.partial(input_kernel, n_mp, first, block, has_total, is_last),
        in_specs=[VMEM] * len(ins),
        out_specs=[VMEM] * len(shapes),
        out_shape=shapes,
        scratch_shapes=scratch,
        compiler_params=params(),
        cost_estimate=cost(30 * rows * deep * count, 8 * rows * deep),
        name="input_share",
    )(*ins)


def pair_kernel(*refs):
    keep_ref, got_ref, outs = refs[0], refs[1], refs[2:]
    for mask in range(len(outs)):
        outs[mask][...] = keep_ref[mask] + got_ref[mask]


def pair_sums(keep, got):
    n, size, deep = keep.shape
    return pl.pallas_call(
        pair_kernel,
        in_specs=[VMEM] * 2,
        out_specs=[VMEM] * n,
        out_shape=[jax.ShapeDtypeStruct((size, deep), F32)] * n,
        compiler_params=params(),
        cost_estimate=cost(0, 12 * n * size * deep),
        name="pair_sums",
    )(keep, got)


def add_kernel(*refs):
    total = refs[0][...]
    for ref in refs[1:-1]:
        total = total + ref[...]
    refs[-1][...] = total


def add_up(parts):
    return pl.pallas_call(
        add_kernel,
        in_specs=[VMEM] * len(parts),
        out_specs=VMEM,
        out_shape=jax.ShapeDtypeStruct(parts[0].shape, F32),
        compiler_params=params(),
        name="add_up",
    )(*parts)


def weight_kernel(n_mp, has_base, t_ref, *refs):
    pieces, out_ref, stack = refs[:n_mp], refs[-2], refs[-1]
    group = pieces[0].shape[0]
    rows = group * n_mp

    @pl.when(pl.program_id(0) == 0)
    def _():
        for mask in range(n_mp):
            high, low = halves(pieces[mask][...])
            for copy, part in enumerate((high, low, high, low)):
                at = copy * rows + mask * group
                stack[at : at + group, :] = part

    out_ref[...] = jnp.dot(t_ref[...], stack[...], preferred_element_type=F32)


def weight_part(turned, pieces, base, index, wide):
    n_mp = len(pieces)
    group, count = pieces[0].shape
    rows, deep = group * n_mp, turned.shape[0]
    block = fit(deep, 256)
    has_base = base is not None
    ins = [turned, *pieces] + ([base] if has_base else [])
    specs = [pl.BlockSpec((block, 4 * rows), lambda i: (i, 0))] + [VMEM] * n_mp
    if has_base:
        specs.append(pl.BlockSpec(memory_space=pl.ANY))
    return pl.pallas_call(
        functools.partial(weight_kernel, n_mp, has_base),
        grid=(deep // block,),
        in_specs=specs,
        out_specs=pl.BlockSpec((block, count), lambda i: (i, index)),
        out_shape=jax.ShapeDtypeStruct((deep, wide), F32),
        scratch_shapes=[pltpu.VMEM((4 * rows, count), BF16)],
        input_output_aliases={len(ins) - 1: 0} if has_base else {},
        compiler_params=params(14),
        cost_estimate=cost(0, 4 * deep * count),
        name="weight_part",
    )(*ins)


def body(inputs, weight, upstream):
    n_mp, n_hid = lax.axis_size("mp"), lax.axis_size("hidden")
    wide = weight.shape[1]
    count = wide // CHUNKS
    starts = [c * count for c in range(CHUNKS)]

    partner = swap(inputs, "hidden", 1)
    even = lax.axis_index("hidden") % 2 == 0
    pair = jnp.concatenate([jnp.where(even, inputs, partner), jnp.where(even, partner, inputs)], axis=0)
    pieces = [pair] + [swap(pair, "hidden", 2 * mask) for mask in range(1, n_hid // 2)]
    high, low = split_weight(weight)
    x = order_rows(pieces, n_mp)
    turned = turn_rows(x)

    parts = [partial_pre(x, high, low, n_mp, first, count) for first in starts]
    mine = []
    for first, own in zip(starts, parts):
        got = [own[0]] + [swap(own[mask], "mp", mask) for mask in range(1, n_mp)]
        mine.append(grad_mine(got, upstream, first))
    grads = [[own] + [swap(own, "mp", mask) for mask in range(1, n_mp)] for own in mine]

    total, weight_grad = None, None
    for c, first in enumerate(starts):
        is_last = c == CHUNKS - 1
        out = input_share(high, low, grads[c], total, first, n_hid, is_last)
        if not is_last:
            total = out[0]
        weight_grad = weight_part(turned, grads[c], weight_grad, c, wide)
    keep, send = out
    sums = pair_sums(keep, swap(send, "hidden", 1))
    input_grad = add_up([sums[0]] + [swap(sums[mask], "hidden", 2 * mask) for mask in range(1, n_hid // 2)])
    return input_grad, weight_grad


def solution(mesh):
    placed = (P("hidden", "mp"), P("mp", "hidden"), P("mp", "hidden"))
    return jax.shard_map(
        body,
        mesh=mesh,
        in_specs=placed,
        out_specs=(P("hidden", "mp"), P("mp", "hidden")),
        check_vma=False,
    )
```

```python
import functools

import jax
import jax.numpy as jnp
from jax import lax
from jax.experimental import pallas as pl
from jax.experimental.pallas import tpu as pltpu
from jax.sharding import PartitionSpec as P

F32, BF16 = jnp.float32, jnp.bfloat16
MIB = 1 << 20
VMEM = pl.BlockSpec(memory_space=pltpu.VMEM)
FIRST = 4
SLOTS = 4


def params(mib=12):
    return pltpu.CompilerParams(vmem_limit_bytes=mib * MIB)


def cost(flops, moved):
    return pl.CostEstimate(flops=int(flops), bytes_accessed=int(moved), transcendentals=0)


def fit(size, block):
    while size % block:
        block //= 2
    return block


def halves(value):
    high = value.astype(BF16)
    return high, (value - high.astype(F32)).astype(BF16)


def swap(value, axis, mask):
    size = lax.axis_size(axis)
    return lax.ppermute(value, axis, [(i, i ^ mask) for i in range(size)])


def load_kernel(n_mp, first, with_pre, w_ref, *refs):
    if with_pre:
        x_ref, refs = refs[0], refs[1:]
    high_ref, low_ref, refs = refs[0], refs[1], refs[2:]
    outs, refs = refs[: len(refs) - 3 if with_pre else 0], refs[-3:] if with_pre else refs[-2:]
    slots, sems = refs[0], refs[1]
    n_slot, block, count = slots.shape
    steps = high_ref.shape[0] // block

    def copy(i, slot):
        at = pl.ds(pl.multiple_of(i * block, block), block)
        return pltpu.make_async_copy(w_ref.at[at, pl.ds(first, count)], slots.at[slot], sems.at[slot])

    for i in range(min(n_slot, steps)):
        copy(i, i).start()
    if with_pre:
        total = refs[2]
        rows = total.shape[0]
        total[...] = jnp.zeros_like(total)

    def step(i, _):
        slot = lax.rem(i, n_slot)
        at = pl.ds(pl.multiple_of(i * block, block), block)
        copy(i, slot).wait()
        high, low = halves(slots[slot])
        high_ref[at, :] = high
        low_ref[at, :] = low

        @pl.when(i + n_slot < steps)
        def _():
            copy(i + n_slot, slot).start()

        if with_pre:
            total[...] += product(x_ref, high_ref, low_ref, at, slice(None))
        return 0

    lax.fori_loop(0, steps, step, 0)
    if with_pre:
        group = rows // n_mp
        for mask in range(n_mp):
            outs[mask][...] = total[mask * group : (mask + 1) * group]


def product(x_ref, high_ref, low_ref, deep, cols):
    rows = x_ref.shape[0] // 2
    both = jnp.dot(x_ref[:, deep], high_ref[deep, cols], preferred_element_type=F32)
    last = jnp.dot(x_ref[:rows, deep], low_ref[deep, cols], preferred_element_type=F32)
    return both[:rows] + both[rows:] + last


def load_weight(weight, first, count, n_mp, x=None):
    deep = weight.shape[0]
    block = fit(deep, 256)
    ins, shapes = [weight], [pltpu.VMEM((deep, count), BF16)] * 2
    specs = [pl.BlockSpec(memory_space=pl.ANY)]
    scratch = [pltpu.VMEM((min(SLOTS, deep // block), block, count), F32), pltpu.SemaphoreType.DMA((SLOTS,))]
    if x is not None:
        rows = x.shape[0] // 2
        ins, specs = ins + [x], specs + [VMEM]
        shapes = shapes + [jax.ShapeDtypeStruct((rows // n_mp, count), F32)] * n_mp
        scratch = scratch + [pltpu.VMEM((rows, count), F32)]
    out = pl.pallas_call(
        functools.partial(load_kernel, n_mp, first, x is not None),
        in_specs=specs,
        out_specs=[VMEM] * len(shapes),
        out_shape=shapes,
        scratch_shapes=scratch,
        compiler_params=params(14),
        cost_estimate=cost(0, 4 * deep * count),
        name="load_weight",
    )(*ins)
    return out[0], out[1], out[2:]


def lay_kernel(*refs):
    refs = refs[1:]
    size = refs[0].shape[0]
    for mask, ref in enumerate(refs[:-1]):
        refs[-1][mask * size : (mask + 1) * size, :] = ref[...]


def lay_rows(pieces, after):
    size, deep = pieces[0].shape
    return pl.pallas_call(
        lay_kernel,
        in_specs=[pl.BlockSpec(memory_space=pl.ANY)] + [VMEM] * len(pieces),
        out_specs=VMEM,
        out_shape=jax.ShapeDtypeStruct((size * len(pieces), deep), F32),
        compiler_params=params(),
        cost_estimate=cost(0, 8 * size * len(pieces) * deep),
        name="lay_rows",
    )(after, *pieces)


def rows_kernel(n_mp, size, own_ref, other_ref, x_ref, flat):
    rows = flat.shape[0]
    hid = lax.axis_index("hidden")
    me = lax.axis_index("mp")
    for mask in range(rows // size // 2):
        own = hid ^ (2 * mask)
        at = slice(mask * size, (mask + 1) * size)
        flat[pl.ds(pl.multiple_of(own * size, size), size), :] = own_ref[at, :]
        flat[pl.ds(pl.multiple_of((own ^ 1) * size, size), size), :] = other_ref[at, :]
    group = rows // n_mp
    for mask in range(n_mp):
        block = flat[pl.ds(pl.multiple_of((me ^ mask) * group, group), group), :]
        high, low = halves(block)
        x_ref[mask * group : (mask + 1) * group, :] = high
        x_ref[rows + mask * group : rows + (mask + 1) * group, :] = low


def order_rows(own, other, n_mp, size):
    rows, deep = 2 * own.shape[0], own.shape[1]
    return pl.pallas_call(
        functools.partial(rows_kernel, n_mp, size),
        in_specs=[VMEM] * 2,
        out_specs=VMEM,
        out_shape=jax.ShapeDtypeStruct((2 * rows, deep), BF16),
        scratch_shapes=[pltpu.VMEM((rows, deep), F32)],
        compiler_params=params(),
        cost_estimate=cost(0, 8 * rows * deep),
        name="order_rows",
    )(own, other)


def turn_kernel(x_ref, t_ref):
    rows = x_ref.shape[0] // 2
    high = x_ref[:rows, :].astype(F32)
    low = x_ref[rows:, :].astype(F32)
    t_ref[...] = jnp.concatenate([high, high, low, low], axis=0).T.astype(BF16)


def turn_rows(x):
    two, deep = x.shape
    return pl.pallas_call(
        turn_kernel,
        in_specs=[VMEM],
        out_specs=VMEM,
        out_shape=jax.ShapeDtypeStruct((deep, 2 * two), BF16),
        compiler_params=params(),
        cost_estimate=cost(0, 4 * two * deep),
        name="turn_rows",
    )(x)


def pre_kernel(n_mp, block, x_ref, high_ref, low_ref, *outs):
    group = x_ref.shape[0] // 2 // n_mp

    def step(j, _):
        here = pl.ds(pl.multiple_of(j * block, block), block)
        total = product(x_ref, high_ref, low_ref, slice(None), here)
        for mask in range(n_mp):
            outs[mask][:, here] = total[mask * group : (mask + 1) * group]
        return 0

    lax.fori_loop(0, outs[0].shape[1] // block, step, 0)


def partial_pre(x, high, low, n_mp):
    rows, deep, count = x.shape[0] // 2, x.shape[1], high.shape[1]
    return pl.pallas_call(
        functools.partial(pre_kernel, n_mp, fit(count, 512)),
        in_specs=[VMEM] * 3,
        out_specs=[VMEM] * n_mp,
        out_shape=[jax.ShapeDtypeStruct((rows // n_mp, count), F32)] * n_mp,
        compiler_params=params(),
        cost_estimate=cost(20 * rows * deep * count, 4 * rows * count),
        name="partial_pre",
    )(x, high, low)


def slope_kernel(first, *refs):
    parts, up_ref, out_ref = refs[:-2], refs[-2], refs[-1]
    pre = parts[0][...]
    for part in parts[1:]:
        pre = pre + part[...]
    cdf = 0.5 * (1.0 + lax.erf(pre * 0.7071067811865476))
    slope = cdf + pre * jnp.exp(-0.5 * pre * pre) * 0.3989422804014327
    out_ref[...] = up_ref[:, first : first + pre.shape[1]] * slope


def grad_mine(parts, upstream, first):
    rows, count = parts[0].shape
    return pl.pallas_call(
        functools.partial(slope_kernel, first),
        in_specs=[VMEM] * (len(parts) + 1),
        out_specs=VMEM,
        out_shape=jax.ShapeDtypeStruct((rows, count), F32),
        compiler_params=params(),
        cost_estimate=cost(0, 24 * rows * count),
        name="grad_mine",
    )(*parts, upstream)


def stacked(pieces):
    return halves(jnp.concatenate([piece[...] for piece in pieces], axis=0))


def grads_kernel(n_mp, block, first, do_input, is_last, do_weight, n_skip, *refs):
    refs = list(refs)

    def take(n):
        head = refs[:n]
        del refs[:n]
        return head

    if do_input:
        high_ref, low_ref = take(2)
        in_pieces = take(n_mp)
        (total_ref,) = take(1) if do_input == 2 else (None,)
    if do_weight:
        (t_ref,) = take(1)
        weight_pieces = take(n_mp)
        take(n_skip)
    if do_input:
        outs = take(2 if is_last else 1)
    if do_weight:
        (out_ref,) = take(1)
    if do_input:
        stack_in, flat = take(2)
    if do_weight:
        slots, sems, stack_weight = take(3)
        n_slot, count = slots.shape[0], slots.shape[2]

    steps = (high_ref if do_input else t_ref).shape[0] // block
    if do_weight:
        high, low = stacked(weight_pieces)
        stack_weight[...] = jnp.concatenate([high, low, high, low], axis=0)
    if do_input:
        high, low = stacked(in_pieces)
        stack_in[...] = jnp.concatenate([high.astype(F32), low.astype(F32)], axis=0).T.astype(BF16)
        rows = high.shape[0]
        group = rows // n_mp
        me = lax.axis_index("mp")
        hid = lax.axis_index("hidden")

    def copy(i, slot):
        at = pl.ds(pl.multiple_of(i * block, block), block)
        return pltpu.make_async_copy(slots.at[slot], out_ref.at[at, pl.ds(first, count)], sems.at[slot])

    def step(i, _):
        here = pl.ds(pl.multiple_of(i * block, block), block)
        if do_weight:
            slot = lax.rem(i, n_slot)

            @pl.when(i >= n_slot)
            def _():
                copy(i - n_slot, slot).wait()

            slots[slot] = jnp.dot(t_ref[here, :], stack_weight[...], preferred_element_type=F32)
            copy(i, slot).start()
        if do_input:
            both = jnp.dot(high_ref[here, :], stack_in[...], preferred_element_type=F32)
            last = jnp.dot(low_ref[here, :], stack_in[:, :rows], preferred_element_type=F32)
            total = (both[:, :rows] + both[:, rows:] + last).T
            if total_ref is not None:
                total = total + total_ref[:, here]
            if not is_last:
                outs[0][:, here] = total
                return 0
            for mask in range(n_mp):
                place = pl.ds(pl.multiple_of((me ^ mask) * group, group), group)
                flat[place, :] = total[mask * group : (mask + 1) * group]
            keep_ref, send_ref = outs
            n_pair, size = keep_ref.shape[0], keep_ref.shape[1]
            for mask in range(n_pair):
                own = hid ^ (2 * mask)
                keep_ref[mask, :, here] = flat[pl.ds(pl.multiple_of(own * size, size), size), :]
                other = own ^ 1
                send_ref[mask, :, here] = flat[pl.ds(pl.multiple_of(other * size, size), size), :]
        return 0

    lax.fori_loop(0, steps, step, 0)
    if do_weight:
        for i in range(max(0, steps - n_slot), steps):
            copy(i, i % n_slot).wait()


def grads(n_hid, input_part=None, is_last=False, weight_part=None):
    ins, specs, shapes, outs, scratch, aliases = [], [], [], [], [], {}
    hbm = pl.BlockSpec(memory_space=pl.ANY)
    first = n_skip = do_input = 0
    if input_part is not None:
        high, low, pieces, total = input_part
        n_mp, (group, count) = len(pieces), pieces[0].shape
        rows, deep = group * n_mp, high.shape[0]
        do_input = 1 if total is None else 2
        ins += [high, low, *pieces] + ([] if total is None else [total])
        specs += [VMEM] * len(ins)
        if is_last:
            shapes += [jax.ShapeDtypeStruct((n_hid // 2, rows // n_hid, deep), F32)] * 2
        else:
            shapes += [jax.ShapeDtypeStruct((rows, deep), F32)]
        outs += [VMEM] * len(shapes)
        block = fit(deep, 256 if weight_part else 512)
        scratch += [pltpu.VMEM((count, 2 * rows), BF16), pltpu.VMEM((rows, block), F32)]
    if weight_part is not None:
        turned, pieces, base, first, wide = weight_part
        n_mp, (group, count) = len(pieces), pieces[0].shape
        rows, deep = group * n_mp, turned.shape[0]
        block = fit(deep, 256)
        slots = min(3, deep // block)
        ins += [turned, *pieces]
        specs += [VMEM] * (n_mp + 1)
        if base is not None:
            aliases = {len(ins): len(shapes)}
            ins, specs, n_skip = ins + [base], specs + [hbm], 1
        shapes += [jax.ShapeDtypeStruct((deep, wide), F32)]
        outs += [hbm]
        scratch += [
            pltpu.VMEM((slots, block, count), F32),
            pltpu.SemaphoreType.DMA((slots,)),
            pltpu.VMEM((4 * rows, count), BF16),
        ]
    return pl.pallas_call(
        functools.partial(grads_kernel, n_mp, block, first, do_input, is_last, weight_part is not None, n_skip),
        in_specs=specs,
        out_specs=outs,
        out_shape=shapes,
        scratch_shapes=scratch,
        input_output_aliases=aliases,
        compiler_params=params(14),
        cost_estimate=cost(0, 4 * deep * count),
        name="grads",
    )(*ins)


def pair_kernel(*refs):
    keep_ref, got_ref, outs = refs[0], refs[1], refs[2:]
    for mask in range(len(outs)):
        outs[mask][...] = keep_ref[mask] + got_ref[mask]


def pair_sums(keep, got):
    n, size, deep = keep.shape
    return pl.pallas_call(
        pair_kernel,
        in_specs=[VMEM] * 2,
        out_specs=[VMEM] * n,
        out_shape=[jax.ShapeDtypeStruct((size, deep), F32)] * n,
        compiler_params=params(),
        cost_estimate=cost(0, 12 * n * size * deep),
        name="pair_sums",
    )(keep, got)


def add_kernel(*refs):
    total = refs[0][...]
    for ref in refs[1:-1]:
        total = total + ref[...]
    refs[-1][...] = total


def add_up(parts):
    return pl.pallas_call(
        add_kernel,
        in_specs=[VMEM] * len(parts),
        out_specs=VMEM,
        out_shape=jax.ShapeDtypeStruct(parts[0].shape, F32),
        compiler_params=params(),
        name="add_up",
    )(*parts)


def body(inputs, weight, upstream):
    n_mp, n_hid = lax.axis_size("mp"), lax.axis_size("hidden")
    wide = weight.shape[1]
    cut = wide * FIRST // 8
    ranges = [(0, cut), (cut, wide - cut)]

    high_a, low_a, _ = load_weight(weight, *ranges[0], n_mp)
    own = lay_rows([inputs] + [swap(inputs, "hidden", 2 * mask) for mask in range(1, n_hid // 2)], high_a)
    x = order_rows(own, swap(own, "hidden", 1), n_mp, inputs.shape[0])
    part_a = partial_pre(x, high_a, low_a, n_mp)
    high_b, low_b, part_b = load_weight(weight, *ranges[1], n_mp, x)
    turned = turn_rows(x)

    grad = []
    for (first, _), own in zip(ranges, (part_a, part_b)):
        got = [own[0]] + [swap(own[mask], "mp", mask) for mask in range(1, n_mp)]
        mine = grad_mine(got, upstream, first)
        grad.append([mine] + [swap(mine, "mp", mask) for mask in range(1, n_mp)])

    (total,) = grads(n_hid, (high_a, low_a, grad[0], None))
    keep, send, weight_grad = grads(
        n_hid, (high_b, low_b, grad[1], total), True, (turned, grad[0], None, 0, wide)
    )
    (weight_grad,) = grads(n_hid, weight_part=(turned, grad[1], weight_grad, cut, wide))
    sums = pair_sums(keep, swap(send, "hidden", 1))
    input_grad = add_up([sums[0]] + [swap(sums[mask], "hidden", 2 * mask) for mask in range(1, n_hid // 2)])
    return input_grad, weight_grad


def solution(mesh):
    placed = (P("hidden", "mp"), P("mp", "hidden"), P("mp", "hidden"))
    return jax.shard_map(
        body,
        mesh=mesh,
        in_specs=placed,
        out_specs=(P("hidden", "mp"), P("mp", "hidden")),
        check_vma=False,
    )
```

```python
import functools

import jax
import jax.numpy as jnp
from jax import lax
from jax.experimental import pallas as pl
from jax.experimental.pallas import tpu as pltpu
from jax.sharding import PartitionSpec as P

F32, BF16 = jnp.float32, jnp.bfloat16
MIB = 1 << 20
VMEM = pl.BlockSpec(memory_space=pltpu.VMEM)
SLOTS = 6
EARLY = 4


def params(mib=12):
    return pltpu.CompilerParams(vmem_limit_bytes=mib * MIB)


def cost(flops, moved):
    return pl.CostEstimate(flops=int(flops), bytes_accessed=int(moved), transcendentals=0)


def fit(size, block):
    while size % block:
        block //= 2
    return block


def halves(value):
    high = value.astype(BF16)
    return high, (value - high.astype(F32)).astype(BF16)


def swap(value, axis, mask):
    size = lax.axis_size(axis)
    return lax.ppermute(value, axis, [(i, i ^ mask) for i in range(size)])


def block_copy(w_ref, held_ref, sems, first, block):
    def copy(i):
        at = pl.ds(pl.multiple_of(i * block, block), block)
        return pltpu.make_async_copy(w_ref.at[at, pl.ds(first, held_ref.shape[1])], held_ref.at[at, :], sems.at[i])

    return copy


def load_kernel(first, block, w_ref, held_ref, sems):
    copy = block_copy(w_ref, held_ref, sems, first, block)
    steps = held_ref.shape[0] // block
    for i in range(steps):
        copy(i).start()
    for i in range(steps):
        copy(i).wait()


def load_weight(weight, first, count):
    deep = weight.shape[0]
    block = fit(deep, 256)
    return pl.pallas_call(
        functools.partial(load_kernel, first, block),
        in_specs=[pl.BlockSpec(memory_space=pl.ANY)],
        out_specs=VMEM,
        out_shape=pltpu.VMEM((deep, count), F32),
        scratch_shapes=[pltpu.SemaphoreType.DMA((deep // block,))],
        compiler_params=params(),
        cost_estimate=cost(0, 4 * deep * count),
        name="load_weight",
    )(weight)


def product(x_ref, w_ref, deep, at, cols=slice(None)):
    rows = x_ref.shape[0] // 2
    high, low = halves(w_ref[at, cols])
    both = jnp.dot(x_ref[:, deep], high, preferred_element_type=F32)
    last = jnp.dot(x_ref[:rows, deep], low, preferred_element_type=F32)
    return both[:rows] + both[rows:] + last


def lay_kernel(*refs):
    refs = refs[1:]
    size = refs[0].shape[0]
    for mask, ref in enumerate(refs[:-1]):
        refs[-1][mask * size : (mask + 1) * size, :] = ref[...]


def lay_rows(pieces, after):
    size, deep = pieces[0].shape
    return pl.pallas_call(
        lay_kernel,
        in_specs=[pl.BlockSpec(memory_space=pl.ANY)] + [VMEM] * len(pieces),
        out_specs=VMEM,
        out_shape=jax.ShapeDtypeStruct((size * len(pieces), deep), F32),
        compiler_params=params(),
        cost_estimate=cost(0, 8 * size * len(pieces) * deep),
        name="lay_rows",
    )(after, *pieces)


def rows_kernel(n_mp, size, own_ref, other_ref, x_ref, flat):
    rows = flat.shape[0]
    hid = lax.axis_index("hidden")
    me = lax.axis_index("mp")
    for mask in range(rows // size // 2):
        own = hid ^ (2 * mask)
        at = slice(mask * size, (mask + 1) * size)
        flat[pl.ds(pl.multiple_of(own * size, size), size), :] = own_ref[at, :]
        flat[pl.ds(pl.multiple_of((own ^ 1) * size, size), size), :] = other_ref[at, :]
    group = rows // n_mp
    for mask in range(n_mp):
        block = flat[pl.ds(pl.multiple_of((me ^ mask) * group, group), group), :]
        high, low = halves(block)
        x_ref[mask * group : (mask + 1) * group, :] = high
        x_ref[rows + mask * group : rows + (mask + 1) * group, :] = low


def order_rows(own, other, n_mp, size):
    rows, deep = 2 * own.shape[0], own.shape[1]
    return pl.pallas_call(
        functools.partial(rows_kernel, n_mp, size),
        in_specs=[VMEM] * 2,
        out_specs=VMEM,
        out_shape=jax.ShapeDtypeStruct((2 * rows, deep), BF16),
        scratch_shapes=[pltpu.VMEM((rows, deep), F32)],
        compiler_params=params(),
        cost_estimate=cost(0, 8 * rows * deep),
        name="order_rows",
    )(own, other)


def turn_kernel(x_ref, t_ref):
    rows = x_ref.shape[0] // 2
    high = x_ref[:rows, :].astype(F32)
    low = x_ref[rows:, :].astype(F32)
    t_ref[...] = jnp.concatenate([high, high, low, low], axis=0).T.astype(BF16)


def turn_rows(x):
    two, deep = x.shape
    return pl.pallas_call(
        turn_kernel,
        in_specs=[VMEM],
        out_specs=VMEM,
        out_shape=jax.ShapeDtypeStruct((deep, 2 * two), BF16),
        compiler_params=params(),
        cost_estimate=cost(0, 4 * two * deep),
        name="turn_rows",
    )(x)


def first_kernel(n_mp, block, first, piece, x_ref, w_ref, all_ref, *refs):
    outs, held_ref, sems = refs[:n_mp], refs[n_mp], refs[n_mp + 1]
    group = x_ref.shape[0] // 2 // n_mp
    copy = block_copy(all_ref, held_ref, sems, first, piece)
    loads = sems.shape[0]
    for i in range(loads):
        copy(i).start()

    def step(j, _):
        here = pl.ds(pl.multiple_of(j * block, block), block)
        total = product(x_ref, w_ref, slice(None), slice(None), here)
        for mask in range(n_mp):
            outs[mask][:, here] = total[mask * group : (mask + 1) * group]
        return 0

    lax.fori_loop(0, outs[0].shape[1] // block, step, 0)
    for i in range(loads):
        copy(i).wait()


def second_kernel(n_mp, first, piece, x_ref, old_ref, all_ref, *refs):
    outs, held_ref, sems, total = refs[:n_mp], refs[n_mp], refs[n_mp + 1], refs[n_mp + 2]
    half = old_ref.shape[0]
    copy = block_copy(all_ref.at[pl.ds(half, held_ref.shape[0]), :], held_ref, sems, first, piece)
    for i in range(sems.shape[0]):
        copy(i).start()
    total[...] = jnp.zeros_like(total)

    def add(base, ref, i):
        at = pl.ds(pl.multiple_of(i * piece, piece), piece)
        deep = pl.ds(pl.multiple_of(base + i * piece, piece), piece)
        total[...] += product(x_ref, ref, deep, at)

    def old_step(i, _):
        add(0, old_ref, i)
        return 0

    def new_step(i, _):
        copy(i).wait()
        add(half, held_ref, i)
        return 0

    lax.fori_loop(0, half // piece, old_step, 0)
    lax.fori_loop(0, held_ref.shape[0] // piece, new_step, 0)
    group = total.shape[0] // n_mp
    for mask in range(n_mp):
        outs[mask][...] = total[mask * group : (mask + 1) * group]


def partial_pre(x, held, weight, first, count, n_mp, is_first):
    rows, deep = x.shape[0] // 2, x.shape[1]
    half = deep // 2
    piece = fit(half, 256)
    width = held.shape[1] if is_first else count
    scratch = [pltpu.SemaphoreType.DMA((half // piece,))]
    if is_first:
        kernel = functools.partial(first_kernel, n_mp, fit(width, 256), first, piece)
    else:
        kernel = functools.partial(second_kernel, n_mp, first, piece)
        scratch = scratch + [pltpu.VMEM((rows, count), F32)]
    out = pl.pallas_call(
        kernel,
        in_specs=[VMEM, VMEM, pl.BlockSpec(memory_space=pl.ANY)],
        out_specs=[VMEM] * (n_mp + 1),
        out_shape=[jax.ShapeDtypeStruct((rows // n_mp, width), F32)] * n_mp + [pltpu.VMEM((half, count), F32)],
        scratch_shapes=scratch,
        compiler_params=params(),
        cost_estimate=cost(20 * rows * deep * width, 4 * rows * width),
        name="partial_pre",
    )(x, held, weight)
    return out[:n_mp], out[n_mp]


def slope_kernel(first, n_parts, *refs):
    parts, up_ref, refs = refs[:n_parts], refs[n_parts], refs[n_parts + 1 :]
    n_pass = len(refs) // 2
    pre = parts[0][...]
    for part in parts[1:]:
        pre = pre + part[...]
    cdf = 0.5 * (1.0 + lax.erf(pre * 0.7071067811865476))
    slope = cdf + pre * jnp.exp(-0.5 * pre * pre) * 0.3989422804014327
    refs[n_pass][...] = up_ref[:, first : first + pre.shape[1]] * slope
    for source, target in zip(refs[:n_pass], refs[n_pass + 1 :]):
        target[...] = source[...]


def grad_mine(parts, upstream, first, passed=()):
    rows, count = parts[0].shape
    out = pl.pallas_call(
        functools.partial(slope_kernel, first, len(parts)),
        in_specs=[VMEM] * (len(parts) + 1 + len(passed)),
        out_specs=[VMEM] * (1 + len(passed)),
        out_shape=[jax.ShapeDtypeStruct((rows, count), F32)] + [jax.ShapeDtypeStruct(p.shape, F32) for p in passed],
        compiler_params=params(),
        cost_estimate=cost(0, 24 * rows * count),
        name="grad_mine",
    )(*parts, upstream, *passed)
    return out[0], list(out[1:])


def stacked(pieces):
    return halves(jnp.concatenate([piece[...] for piece in pieces], axis=0))


def input_kernel(n_mp, n_weight, block, has_total, is_last, *refs):
    w_refs, pieces, refs = refs[:n_weight], refs[n_weight : n_weight + n_mp], refs[n_weight + n_mp :]
    total_ref, outs, (stack, flat) = refs[0] if has_total else None, refs[has_total:-2], refs[-2:]
    high, low = stacked(pieces)
    stack[...] = jnp.concatenate([high.astype(F32), low.astype(F32)], axis=0).T.astype(BF16)
    rows = high.shape[0]
    group = rows // n_mp
    me = lax.axis_index("mp")
    hid = lax.axis_index("hidden")

    def step(w_ref, base, i):
        here = pl.ds(pl.multiple_of(base + i * block, block), block)
        high, low = halves(w_ref[pl.ds(pl.multiple_of(i * block, block), block), :])
        both = jnp.dot(high, stack[...], preferred_element_type=F32)
        last = jnp.dot(low, stack[:, :rows], preferred_element_type=F32)
        total = (both[:, :rows] + both[:, rows:] + last).T
        if total_ref is not None:
            total = total + total_ref[:, here]
        if not is_last:
            outs[0][:, here] = total
            return 0
        for mask in range(n_mp):
            place = pl.ds(pl.multiple_of((me ^ mask) * group, group), group)
            flat[place, :] = total[mask * group : (mask + 1) * group]
        keep_ref, send_ref = outs
        n_pair, size = keep_ref.shape[0], keep_ref.shape[1]
        for mask in range(n_pair):
            own = hid ^ (2 * mask)
            keep_ref[mask, :, here] = flat[pl.ds(pl.multiple_of(own * size, size), size), :]
            other = own ^ 1
            send_ref[mask, :, here] = flat[pl.ds(pl.multiple_of(other * size, size), size), :]
        return 0

    base = 0
    for w_ref in w_refs:
        lax.fori_loop(0, w_ref.shape[0] // block, lambda i, _, w=w_ref, at=base: step(w, at, i), 0)
        base += w_ref.shape[0]


def input_share(weights, pieces, total, n_hid, is_last):
    n_mp, (group, count) = len(pieces), pieces[0].shape
    rows, deep = group * n_mp, sum(w.shape[0] for w in weights)
    block = fit(weights[0].shape[0], 1024)
    ins = [*weights, *pieces] + ([] if total is None else [total])
    if is_last:
        shapes = [jax.ShapeDtypeStruct((n_hid // 2, rows // n_hid, deep), F32)] * 2
    else:
        shapes = [jax.ShapeDtypeStruct((rows, deep), F32)]
    return pl.pallas_call(
        functools.partial(input_kernel, n_mp, len(weights), block, int(total is not None), is_last),
        in_specs=[VMEM] * len(ins),
        out_specs=[VMEM] * len(shapes),
        out_shape=shapes,
        scratch_shapes=[pltpu.VMEM((count, 2 * rows), BF16), pltpu.VMEM((rows, block), F32)],
        compiler_params=params(14),
        cost_estimate=cost(20 * rows * deep * count, 4 * rows * deep),
        name="input_share",
    )(*ins)


def weight_kernel(n_mp, part, jobs, n_skip, t_ref, *refs):
    groups, refs = [refs[j * n_mp : (j + 1) * n_mp] for j in range(len(jobs))], refs[len(jobs) * n_mp + n_skip :]
    out_ref, mark_ref, slots, sems, stacks = refs
    mark_ref[...] = jnp.zeros_like(mark_ref)
    n_slot, count = slots.shape[0], slots.shape[2]

    def copy(i, first, row):
        slot = lax.rem(i, n_slot)
        at = pl.ds(pl.multiple_of(row, part), part)
        return pltpu.make_async_copy(slots.at[slot], out_ref.at[at, pl.ds(first, count)], sems.at[slot])

    done = 0
    for j, (first, start, end) in enumerate(jobs):
        high, low = stacked(groups[j])
        stacks[j] = jnp.concatenate([high, low, high, low], axis=0)

        def step(i, _, j=j, first=first, start=start, base=done):
            turn = base + i

            @pl.when(turn >= n_slot)
            def _():
                copy(turn, first, start).wait()

            row = start + i * part
            at = pl.ds(pl.multiple_of(row, part), part)
            slots[lax.rem(turn, n_slot)] = jnp.dot(t_ref[at, :], stacks[j], preferred_element_type=F32)
            copy(turn, first, row).start()
            return 0

        lax.fori_loop(0, (end - start) // part, step, 0)
        done += (end - start) // part
    for i in range(max(0, done - n_slot), done):
        copy(i, jobs[-1][0], jobs[-1][1]).wait()


def weight_part(turned, jobs, part, base, after, wide):
    pieces = [piece for job in jobs for piece in job[0]]
    n_mp, (group, count) = len(jobs[0][0]), pieces[0].shape
    rows, deep = group * n_mp, turned.shape[0]
    skipped = [after] if base is None else [after, base]
    ins = [turned, *pieces, *skipped]
    return pl.pallas_call(
        functools.partial(weight_kernel, n_mp, part, [job[1:] for job in jobs], len(skipped)),
        in_specs=[VMEM] * (1 + len(pieces)) + [pl.BlockSpec(memory_space=pl.ANY)] * len(skipped),
        out_specs=[pl.BlockSpec(memory_space=pl.ANY), VMEM],
        out_shape=[jax.ShapeDtypeStruct((deep, wide), F32), jax.ShapeDtypeStruct((8, 128), F32)],
        scratch_shapes=[
            pltpu.VMEM((SLOTS, part, count), F32),
            pltpu.SemaphoreType.DMA((SLOTS,)),
            pltpu.VMEM((len(jobs), 4 * rows, count), BF16),
        ],
        input_output_aliases={} if base is None else {len(ins) - 1: 0},
        compiler_params=params(14),
        cost_estimate=cost(0, 4 * count * sum(job[3] - job[2] for job in jobs)),
        name="weight_part",
    )(*ins)


def pair_kernel(*refs):
    keep_ref, got_ref, outs = refs[0], refs[1], refs[3:]
    for mask in range(len(outs)):
        outs[mask][...] = keep_ref[mask] + got_ref[mask]


def pair_sums(keep, got, after):
    n, size, deep = keep.shape
    return pl.pallas_call(
        pair_kernel,
        in_specs=[VMEM] * 2 + [pl.BlockSpec(memory_space=pl.ANY)],
        out_specs=[VMEM] * n,
        out_shape=[jax.ShapeDtypeStruct((size, deep), F32)] * n,
        compiler_params=params(),
        cost_estimate=cost(0, 12 * n * size * deep),
        name="pair_sums",
    )(keep, got, after)


def add_kernel(*refs):
    total = refs[0][...]
    for ref in refs[1:-1]:
        total = total + ref[...]
    refs[-1][...] = total


def add_up(parts):
    return pl.pallas_call(
        add_kernel,
        in_specs=[VMEM] * len(parts),
        out_specs=VMEM,
        out_shape=jax.ShapeDtypeStruct(parts[0].shape, F32),
        compiler_params=params(),
        name="add_up",
    )(*parts)


def body(inputs, weight, upstream):
    n_mp, n_hid = lax.axis_size("mp"), lax.axis_size("hidden")
    wide = weight.shape[1]
    cut = wide // 2
    ranges = [(0, cut), (cut, wide - cut)]

    held_a = load_weight(weight, 0, cut)
    own = lay_rows([inputs] + [swap(inputs, "hidden", 2 * mask) for mask in range(1, n_hid // 2)], held_a)
    x = order_rows(own, swap(own, "hidden", 1), n_mp, inputs.shape[0])
    part_a, held_b = partial_pre(x, held_a, weight, *ranges[1], n_mp, True)
    part_b, held_c = partial_pre(x, held_b, weight, *ranges[1], n_mp, False)
    turned = turn_rows(x)

    def exchange(own):
        return [own[0]] + [swap(own[mask], "mp", mask) for mask in range(1, n_mp)]

    got_a = exchange(part_a)
    mine_a, _ = grad_mine(got_a, upstream, 0)
    mine_b, _ = grad_mine(exchange(part_b), upstream, cut)
    grad_a, grad_b = [[mine] + [swap(mine, "mp", mask) for mask in range(1, n_mp)] for mine in (mine_a, mine_b)]

    (total,) = input_share([held_a], grad_a, None, n_hid, False)
    keep, send = input_share([held_b, held_c], grad_b, total, n_hid, True)
    deep = turned.shape[0]
    part = fit(deep // 4, 128)
    early = part * max(1, deep // part * EARLY // 16)
    weight_grad, mark = weight_part(turned, [(grad_a, 0, 0, early)], part, None, keep, wide)
    sums = pair_sums(keep, swap(send, "hidden", 1), mark)
    jobs = [(grad_a, 0, early, deep), (grad_b, cut, 0, deep)]
    weight_grad, _ = weight_part(turned, jobs, part, weight_grad, sums[0], wide)
    input_grad = add_up([sums[0]] + [swap(sums[mask], "hidden", 2 * mask) for mask in range(1, n_hid // 2)])
    return input_grad, weight_grad


def solution(mesh):
    placed = (P("hidden", "mp"), P("mp", "hidden"), P("mp", "hidden"))
    return jax.shard_map(
        body,
        mesh=mesh,
        in_specs=placed,
        out_specs=(P("hidden", "mp"), P("mp", "hidden")),
        check_vma=False,
    )
```

```python
import functools

import jax
import jax.numpy as jnp
from jax import lax
from jax.experimental import pallas as pl
from jax.experimental.pallas import tpu as pltpu
from jax.sharding import PartitionSpec as P

F32, BF16 = jnp.float32, jnp.bfloat16
MIB = 1 << 20
VMEM = pl.BlockSpec(memory_space=pltpu.VMEM)
SLOTS = 6
EARLY = 4


def params(mib=12):
    return pltpu.CompilerParams(vmem_limit_bytes=mib * MIB)


def cost(flops, moved):
    return pl.CostEstimate(flops=int(flops), bytes_accessed=int(moved), transcendentals=0)


def fit(size, block):
    while size % block:
        block //= 2
    return block


def halves(value):
    high = value.astype(BF16)
    return high, (value - high.astype(F32)).astype(BF16)


def swap(value, axis, mask):
    size = lax.axis_size(axis)
    return lax.ppermute(value, axis, [(i, i ^ mask) for i in range(size)])


def block_copy(w_ref, held_ref, sems, first, block):
    def copy(i):
        at = pl.ds(pl.multiple_of(i * block, block), block)
        return pltpu.make_async_copy(w_ref.at[at, pl.ds(first, held_ref.shape[1])], held_ref.at[at, :], sems.at[i])

    return copy


def load_kernel(first, block, w_ref, held_ref, sems):
    copy = block_copy(w_ref, held_ref, sems, first, block)
    steps = held_ref.shape[0] // block
    for i in range(steps):
        copy(i).start()
    for i in range(steps):
        copy(i).wait()


def load_weight(weight, first, count):
    deep = weight.shape[0]
    block = fit(deep, 256)
    return pl.pallas_call(
        functools.partial(load_kernel, first, block),
        in_specs=[pl.BlockSpec(memory_space=pl.ANY)],
        out_specs=VMEM,
        out_shape=pltpu.VMEM((deep, count), F32),
        scratch_shapes=[pltpu.SemaphoreType.DMA((deep // block,))],
        compiler_params=params(),
        cost_estimate=cost(0, 4 * deep * count),
        name="load_weight",
    )(weight)


def product(x_ref, w_ref, deep, at, cols=slice(None)):
    rows = x_ref.shape[0] // 2
    high, low = halves(w_ref[at, cols])
    both = jnp.dot(x_ref[:, deep], high, preferred_element_type=F32)
    last = jnp.dot(x_ref[:rows, deep], low, preferred_element_type=F32)
    return both[:rows] + both[rows:] + last


def lay_kernel(*refs):
    refs = refs[1:]
    size = refs[0].shape[0]
    for mask, ref in enumerate(reversed(refs[:-1])):
        refs[-1][mask * size : (mask + 1) * size, :] = ref[...]


def lay_rows(pieces, after):
    size, deep = pieces[0].shape
    return pl.pallas_call(
        lay_kernel,
        in_specs=[pl.BlockSpec(memory_space=pl.ANY)] + [VMEM] * len(pieces),
        out_specs=VMEM,
        out_shape=jax.ShapeDtypeStruct((size * len(pieces), deep), F32),
        compiler_params=params(),
        cost_estimate=cost(0, 8 * size * len(pieces) * deep),
        name="lay_rows",
    )(after, *pieces)


def rows_kernel(n_mp, size, own_ref, other_ref, x_ref, flat):
    rows = flat.shape[0]
    hid = lax.axis_index("hidden")
    me = lax.axis_index("mp")
    for mask in range(rows // size // 2):
        own = hid ^ (2 * mask)
        at = slice(mask * size, (mask + 1) * size)
        flat[pl.ds(pl.multiple_of(own * size, size), size), :] = own_ref[at, :]
        flat[pl.ds(pl.multiple_of((own ^ 1) * size, size), size), :] = other_ref[at, :]
    group = rows // n_mp
    for mask in range(n_mp):
        block = flat[pl.ds(pl.multiple_of((me ^ mask) * group, group), group), :]
        high, low = halves(block)
        x_ref[mask * group : (mask + 1) * group, :] = high
        x_ref[rows + mask * group : rows + (mask + 1) * group, :] = low


def order_rows(own, other, n_mp, size):
    rows, deep = 2 * own.shape[0], own.shape[1]
    return pl.pallas_call(
        functools.partial(rows_kernel, n_mp, size),
        in_specs=[VMEM] * 2,
        out_specs=VMEM,
        out_shape=jax.ShapeDtypeStruct((2 * rows, deep), BF16),
        scratch_shapes=[pltpu.VMEM((rows, deep), F32)],
        compiler_params=params(),
        cost_estimate=cost(0, 8 * rows * deep),
        name="order_rows",
    )(own, other)


def turn_kernel(x_ref, t_ref):
    rows = x_ref.shape[0] // 2
    high = x_ref[:rows, :].astype(F32)
    low = x_ref[rows:, :].astype(F32)
    t_ref[...] = jnp.concatenate([high, high, low, low], axis=0).T.astype(BF16)


def turn_rows(x):
    two, deep = x.shape
    return pl.pallas_call(
        turn_kernel,
        in_specs=[VMEM],
        out_specs=VMEM,
        out_shape=jax.ShapeDtypeStruct((deep, 2 * two), BF16),
        compiler_params=params(),
        cost_estimate=cost(0, 4 * two * deep),
        name="turn_rows",
    )(x)


def first_kernel(n_mp, block, first, piece, x_ref, w_ref, all_ref, *refs):
    outs, held_ref, sems = refs[:n_mp], refs[n_mp], refs[n_mp + 1]
    group = x_ref.shape[0] // 2 // n_mp
    copy = block_copy(all_ref, held_ref, sems, first, piece)
    loads = sems.shape[0]
    for i in range(loads):
        copy(i).start()

    def step(j, _):
        here = pl.ds(pl.multiple_of(j * block, block), block)
        total = product(x_ref, w_ref, slice(None), slice(None), here)
        for mask in range(n_mp):
            outs[mask][:, here] = total[mask * group : (mask + 1) * group]
        return 0

    lax.fori_loop(0, outs[0].shape[1] // block, step, 0)
    for i in range(loads):
        copy(i).wait()


def second_kernel(n_mp, first, piece, x_ref, old_ref, all_ref, *refs):
    outs, held_ref, sems, total = refs[:n_mp], refs[n_mp], refs[n_mp + 1], refs[n_mp + 2]
    half = old_ref.shape[0]
    copy = block_copy(all_ref.at[pl.ds(half, held_ref.shape[0]), :], held_ref, sems, first, piece)
    for i in range(sems.shape[0]):
        copy(i).start()
    total[...] = jnp.zeros_like(total)

    def add(base, ref, i):
        at = pl.ds(pl.multiple_of(i * piece, piece), piece)
        deep = pl.ds(pl.multiple_of(base + i * piece, piece), piece)
        total[...] += product(x_ref, ref, deep, at)

    def old_step(i, _):
        add(0, old_ref, i)
        return 0

    def new_step(i, _):
        copy(i).wait()
        add(half, held_ref, i)
        return 0

    lax.fori_loop(0, half // piece, old_step, 0)
    lax.fori_loop(0, held_ref.shape[0] // piece, new_step, 0)
    group = total.shape[0] // n_mp
    for mask in range(n_mp):
        outs[mask][...] = total[mask * group : (mask + 1) * group]


def partial_pre(x, held, weight, first, count, n_mp, is_first):
    rows, deep = x.shape[0] // 2, x.shape[1]
    half = deep // 2
    piece = fit(half, 256)
    width = held.shape[1] if is_first else count
    scratch = [pltpu.SemaphoreType.DMA((half // piece,))]
    if is_first:
        kernel = functools.partial(first_kernel, n_mp, fit(width, 256), first, piece)
    else:
        kernel = functools.partial(second_kernel, n_mp, first, piece)
        scratch = scratch + [pltpu.VMEM((rows, count), F32)]
    out = pl.pallas_call(
        kernel,
        in_specs=[VMEM, VMEM, pl.BlockSpec(memory_space=pl.ANY)],
        out_specs=[VMEM] * (n_mp + 1),
        out_shape=[jax.ShapeDtypeStruct((rows // n_mp, width), F32)] * n_mp + [pltpu.VMEM((half, count), F32)],
        scratch_shapes=scratch,
        compiler_params=params(),
        cost_estimate=cost(20 * rows * deep * width, 4 * rows * width),
        name="partial_pre",
    )(x, held, weight)
    return out[:n_mp], out[n_mp]


def slope_kernel(first, n_parts, *refs):
    parts, up_ref, refs = refs[:n_parts], refs[n_parts], refs[n_parts + 1 :]
    n_pass = len(refs) // 2
    pre = parts[0][...]
    for part in parts[1:]:
        pre = pre + part[...]
    cdf = 0.5 * (1.0 + lax.erf(pre * 0.7071067811865476))
    slope = cdf + pre * jnp.exp(-0.5 * pre * pre) * 0.3989422804014327
    refs[n_pass][...] = up_ref[:, first : first + pre.shape[1]] * slope
    for source, target in zip(refs[:n_pass], refs[n_pass + 1 :]):
        target[...] = source[...]


def grad_mine(parts, upstream, first, passed=()):
    rows, count = parts[0].shape
    out = pl.pallas_call(
        functools.partial(slope_kernel, first, len(parts)),
        in_specs=[VMEM] * (len(parts) + 1 + len(passed)),
        out_specs=[VMEM] * (1 + len(passed)),
        out_shape=[jax.ShapeDtypeStruct((rows, count), F32)] + [jax.ShapeDtypeStruct(p.shape, F32) for p in passed],
        compiler_params=params(),
        cost_estimate=cost(0, 24 * rows * count),
        name="grad_mine",
    )(*parts, upstream, *passed)
    return out[0], list(out[1:])


def stacked(pieces):
    return halves(jnp.concatenate([piece[...] for piece in pieces], axis=0))


def input_kernel(n_mp, n_weight, block, has_total, is_last, *refs):
    w_refs, pieces, refs = refs[:n_weight], refs[n_weight : n_weight + n_mp], refs[n_weight + n_mp :]
    total_ref, outs, (stack, flat) = refs[0] if has_total else None, refs[has_total:-2], refs[-2:]
    high, low = stacked(pieces)
    stack[...] = jnp.concatenate([high.astype(F32), low.astype(F32)], axis=0).T.astype(BF16)
    rows = high.shape[0]
    group = rows // n_mp
    me = lax.axis_index("mp")
    hid = lax.axis_index("hidden")

    def step(w_ref, base, i):
        here = pl.ds(pl.multiple_of(base + i * block, block), block)
        high, low = halves(w_ref[pl.ds(pl.multiple_of(i * block, block), block), :])
        both = jnp.dot(high, stack[...], preferred_element_type=F32)
        last = jnp.dot(low, stack[:, :rows], preferred_element_type=F32)
        total = (both[:, :rows] + both[:, rows:] + last).T
        if total_ref is not None:
            total = total + total_ref[:, here]
        if not is_last:
            outs[0][:, here] = total
            return 0
        for mask in range(n_mp):
            place = pl.ds(pl.multiple_of((me ^ mask) * group, group), group)
            flat[place, :] = total[mask * group : (mask + 1) * group]
        keep_ref, send_ref = outs
        n_pair, size = keep_ref.shape[0], keep_ref.shape[1]
        for mask in range(n_pair):
            own = hid ^ (2 * mask)
            keep_ref[mask, :, here] = flat[pl.ds(pl.multiple_of(own * size, size), size), :]
            other = own ^ 1
            send_ref[mask, :, here] = flat[pl.ds(pl.multiple_of(other * size, size), size), :]
        return 0

    base = 0
    for w_ref in w_refs:
        lax.fori_loop(0, w_ref.shape[0] // block, lambda i, _, w=w_ref, at=base: step(w, at, i), 0)
        base += w_ref.shape[0]


def input_share(weights, pieces, total, n_hid, is_last):
    n_mp, (group, count) = len(pieces), pieces[0].shape
    rows, deep = group * n_mp, sum(w.shape[0] for w in weights)
    block = fit(weights[0].shape[0], 1024)
    ins = [*weights, *pieces] + ([] if total is None else [total])
    if is_last:
        shapes = [jax.ShapeDtypeStruct((n_hid // 2, rows // n_hid, deep), F32)] * 2
    else:
        shapes = [jax.ShapeDtypeStruct((rows, deep), F32)]
    return pl.pallas_call(
        functools.partial(input_kernel, n_mp, len(weights), block, int(total is not None), is_last),
        in_specs=[VMEM] * len(ins),
        out_specs=[VMEM] * len(shapes),
        out_shape=shapes,
        scratch_shapes=[pltpu.VMEM((count, 2 * rows), BF16), pltpu.VMEM((rows, block), F32)],
        compiler_params=params(14),
        cost_estimate=cost(20 * rows * deep * count, 4 * rows * deep),
        name="input_share",
    )(*ins)


def weight_kernel(n_mp, part, jobs, n_skip, t_ref, *refs):
    groups, refs = [refs[j * n_mp : (j + 1) * n_mp] for j in range(len(jobs))], refs[len(jobs) * n_mp + n_skip :]
    out_ref, mark_ref, slots, sems, stacks = refs
    mark_ref[...] = jnp.zeros_like(mark_ref)
    n_slot, count = slots.shape[0], slots.shape[2]

    def copy(i, first, row):
        slot = lax.rem(i, n_slot)
        at = pl.ds(pl.multiple_of(row, part), part)
        return pltpu.make_async_copy(slots.at[slot], out_ref.at[at, pl.ds(first, count)], sems.at[slot])

    done = 0
    for j, (first, start, end) in enumerate(jobs):
        high, low = stacked(groups[j])
        stacks[j] = jnp.concatenate([high, low, high, low], axis=0)

        def step(i, _, j=j, first=first, start=start, base=done):
            turn = base + i

            @pl.when(turn >= n_slot)
            def _():
                copy(turn, first, start).wait()

            row = start + i * part
            at = pl.ds(pl.multiple_of(row, part), part)
            slots[lax.rem(turn, n_slot)] = jnp.dot(t_ref[at, :], stacks[j], preferred_element_type=F32)
            copy(turn, first, row).start()
            return 0

        lax.fori_loop(0, (end - start) // part, step, 0)
        done += (end - start) // part
    for i in range(max(0, done - n_slot), done):
        copy(i, jobs[-1][0], jobs[-1][1]).wait()


def weight_part(turned, jobs, part, base, after, wide):
    pieces = [piece for job in jobs for piece in job[0]]
    n_mp, (group, count) = len(jobs[0][0]), pieces[0].shape
    rows, deep = group * n_mp, turned.shape[0]
    skipped = [after] if base is None else [after, base]
    ins = [turned, *pieces, *skipped]
    return pl.pallas_call(
        functools.partial(weight_kernel, n_mp, part, [job[1:] for job in jobs], len(skipped)),
        in_specs=[VMEM] * (1 + len(pieces)) + [pl.BlockSpec(memory_space=pl.ANY)] * len(skipped),
        out_specs=[pl.BlockSpec(memory_space=pl.ANY), VMEM],
        out_shape=[jax.ShapeDtypeStruct((deep, wide), F32), jax.ShapeDtypeStruct((8, 128), F32)],
        scratch_shapes=[
            pltpu.VMEM((SLOTS, part, count), F32),
            pltpu.SemaphoreType.DMA((SLOTS,)),
            pltpu.VMEM((len(jobs), 4 * rows, count), BF16),
        ],
        input_output_aliases={} if base is None else {len(ins) - 1: 0},
        compiler_params=params(14),
        cost_estimate=cost(0, 4 * count * sum(job[3] - job[2] for job in jobs)),
        name="weight_part",
    )(*ins)


def pair_kernel(*refs):
    keep_ref, got_ref, outs = refs[0], refs[1], refs[3:]
    for mask in range(len(outs)):
        outs[mask][...] = keep_ref[mask] + got_ref[mask]


def pair_sums(keep, got, after):
    n, size, deep = keep.shape
    return pl.pallas_call(
        pair_kernel,
        in_specs=[VMEM] * 2 + [pl.BlockSpec(memory_space=pl.ANY)],
        out_specs=[VMEM] * n,
        out_shape=[jax.ShapeDtypeStruct((size, deep), F32)] * n,
        compiler_params=params(),
        cost_estimate=cost(0, 12 * n * size * deep),
        name="pair_sums",
    )(keep, got, after)


def add_kernel(*refs):
    total = refs[0][...]
    for ref in refs[1:-1]:
        total = total + ref[...]
    refs[-1][...] = total


def add_up(parts):
    return pl.pallas_call(
        add_kernel,
        in_specs=[VMEM] * len(parts),
        out_specs=VMEM,
        out_shape=jax.ShapeDtypeStruct(parts[0].shape, F32),
        compiler_params=params(),
        name="add_up",
    )(*parts)


def body(inputs, weight, upstream):
    n_mp, n_hid = lax.axis_size("mp"), lax.axis_size("hidden")
    wide = weight.shape[1]
    cut = wide // 2
    ranges = [(0, cut), (cut, wide - cut)]

    held_a = load_weight(weight, 0, cut)
    own = lay_rows([swap(inputs, "hidden", 2 * mask) for mask in range(n_hid // 2 - 1, 0, -1)] + [inputs], held_a)
    x = order_rows(own, swap(own, "hidden", 1), n_mp, inputs.shape[0])
    part_a, held_b = partial_pre(x, held_a, weight, *ranges[1], n_mp, True)
    part_b, held_c = partial_pre(x, held_b, weight, *ranges[1], n_mp, False)
    turned = turn_rows(x)

    def exchange(own):
        return [own[0]] + [swap(own[mask], "mp", mask) for mask in range(1, n_mp)]

    got_a = exchange(part_a)
    mine_a, _ = grad_mine(got_a, upstream, 0)
    mine_b, _ = grad_mine(exchange(part_b), upstream, cut)
    grad_a, grad_b = [[mine] + [swap(mine, "mp", mask) for mask in range(1, n_mp)] for mine in (mine_a, mine_b)]

    (total,) = input_share([held_a], grad_a, None, n_hid, False)
    keep, send = input_share([held_b, held_c], grad_b, total, n_hid, True)
    deep = turned.shape[0]
    part = fit(deep // 4, 128)
    early = part * max(1, deep // part * EARLY // 16)
    weight_grad, mark = weight_part(turned, [(grad_a, 0, 0, early)], part, None, keep, wide)
    sums = pair_sums(keep, swap(send, "hidden", 1), mark)
    jobs = [(grad_a, 0, early, deep), (grad_b, cut, 0, deep)]
    weight_grad, _ = weight_part(turned, jobs, part, weight_grad, sums[0], wide)
    input_grad = add_up([swap(sums[mask], "hidden", 2 * mask) for mask in range(n_hid // 2 - 1, 0, -1)] + [sums[0]])
    return input_grad, weight_grad


def solution(mesh):
    placed = (P("hidden", "mp"), P("mp", "hidden"), P("mp", "hidden"))
    return jax.shard_map(
        body,
        mesh=mesh,
        in_specs=placed,
        out_specs=(P("hidden", "mp"), P("mp", "hidden")),
        check_vma=False,
    )
```
